32 devices in a mesh: row: 2 (over y), col: 4 (over z), vc: 4 (over x, core).
Axes of the slice: x: 2, y: 2, z: 4, core: 2. Of those that a mesh axis runs over, the one named last changes fastest.
Arguments:
- amplitudes: bfloat16 [8, 8, 128, 128], P('row', 'col'), may hold values from -6 to 6
- factors: bfloat16 [2, 4, 256, 128, 128], P('row', 'col', 'vc'), may hold values from -0.125 to 0.125
- pno_counts: int32 [8, 8], P('row', 'col'), may hold values from 32 to 128, as said below
- pair_live: int32 [8, 8], P('row', 'col'), may hold values from 0 to 1, as said below
Outputs:
- residual_ladder: float32 [8, 8, 128, 128], P('row', 'col', 'vc')
The draws below stay inside these ranges and needn't reach their ends.
Inputs may be any that keep to these rules, and one draw needn't show every extreme that they name: pno_counts[i, j] equals pno_counts[j, i]; every diagonal entry is 128. pair_live[i, j] equals pair_live[j, i]; every diagonal entry is 1.
All inputs are finite; a program needn't handle non-finite values.
Results may differ from the reference program's by a relative error of at most 0.0028.
Values sent between devices are 32-bit elements; how exact they have to be, the bound alone decides.
No kernel may reach another device: no remote copies, remote signals or barrier semaphores. Data moves between devices by JAX's collectives and lax.ppermute only.
A program may use at most 64 MiB of HBM per device.

```python
import jax
import jax.numpy as jnp
from jax import lax

NV = 128
NAUX = 256
NO = 8


def draw_pno_counts(key, part):
    key = jax.random.fold_in(key, 11)
    drawn = jax.random.randint(key, (NO, NO), NV // 4, NV + 1)
    row_ids = lax.broadcasted_iota(jnp.int32, (NO, NO), 0)
    col_ids = lax.broadcasted_iota(jnp.int32, (NO, NO), 1)
    symmetric = jnp.where(row_ids <= col_ids, drawn, drawn.T)
    symmetric = jnp.where(row_ids == col_ids, NV, symmetric)
    lowest_pair = (row_ids == 0) & (col_ids == 1) | (row_ids == 1) & (col_ids == 0)
    return jnp.where(lowest_pair, NV // 4, symmetric).astype(jnp.int32)


def draw_pair_live(key, part):
    key = jax.random.fold_in(key, 23)
    drawn = jax.random.randint(key, (NO, NO), 0, 4)
    row_ids = lax.broadcasted_iota(jnp.int32, (NO, NO), 0)
    col_ids = lax.broadcasted_iota(jnp.int32, (NO, NO), 1)
    symmetric = jnp.where(row_ids <= col_ids, drawn, drawn.T)
    flags = jnp.where(symmetric > 0, 1, 0)
    return jnp.where(row_ids == col_ids, 1, flags).astype(jnp.int32)


def levels(rng, dims, pieces, smallest, high):
    def one(axis_at, parts):
        draws = jax.random.uniform(jax.random.fold_in(jax.random.fold_in(rng, 6), axis_at), (parts,), jnp.float32, smallest / len(pieces), high / len(pieces))
        return jnp.repeat(jnp.exp(draws), dims[axis_at] // parts).reshape((-1,) + (1,) * (len(dims) - axis_at - 1))

    level = one(*pieces[0])
    for cut in pieces[1:]:
        level = level * one(*cut)
    return level


def centred(key, dims, scale, bound, split=(), kind=jnp.bfloat16):
    gain = levels(key, dims, split, -0.22, 0.18) if split else 1.0
    result = jax.random.normal(key, dims, jnp.float32) * scale * gain
    return jnp.minimum(jnp.maximum(result, -bound), bound).astype(kind)


def setup_inputs(seed: int = 0) -> dict:
    streams_of = jax.random.split(jax.random.key(seed), 5)
    return {
        "amplitudes": centred(streams_of[0], (NO, NO, NV, NV), 1.0, 6.0, ((0, 2), (1, 4))),
        "factors": centred(streams_of[1], (NO // 4, NO // 2, NAUX, NV, NV), (NV * max(NAUX // 16, 4)) ** -0.5, 0.125, ((0, 2), (1, 4), (2, 4))),
        "pno_counts": draw_pno_counts(jax.random.fold_in(streams_of[4], 71), 0),
        "pair_live": draw_pair_live(jax.random.fold_in(streams_of[4], 71), 0),
    }


def reference(amplitudes, factors, pno_counts, pair_live):
    positions = jnp.arange(NV, dtype=jnp.int32)
    inside = positions[None, None, :] < pno_counts[:, :, None]

    def one_pair(pair_index):
        row_occ = pair_index // NO
        col_occ = pair_index % NO
        domain = factors[row_occ // 4, col_occ // 2].astype(jnp.float32)
        weight_in = inside[row_occ, col_occ].astype(jnp.bfloat16)
        masked = amplitudes[row_occ, col_occ] * weight_in[:, None] * weight_in[None, :]
        half_tile = jnp.einsum("qac,cd->qad", domain, masked.astype(jnp.float32), precision=lax.Precision.HIGHEST).astype(jnp.bfloat16)
        return jnp.einsum("qad,qbd->ab", half_tile.astype(jnp.float32), domain, precision=lax.Precision.HIGHEST)

    ladder = lax.map(one_pair, jnp.arange(NO * NO, dtype=jnp.int32)).reshape(NO, NO, NV, NV)
    combined = ladder + jnp.transpose(ladder, (1, 0, 3, 2))
    kept_cells = inside[:, :, :, None] & inside[:, :, None, :] & (pair_live[:, :, None, None] > 0)
    return jnp.where(kept_cells, combined, jnp.zeros_like(combined))
```

```python
import functools
import math

import jax
import jax.numpy as jnp
from jax import lax
from jax.experimental import pallas as pl
from jax.experimental.pallas import tpu as pltpu
from jax.sharding import PartitionSpec as P

AXES = ("row", "col", "vc")
CORES = 2
Q_BLOCK = 16
ROWS_LAST = (((1,), (1,)), ((), ()))


def add_blocks(first, last, domain, masked, total, half_a, half_b, loaded=None):
    virtuals = domain.shape[1]
    pairs = total.shape[0] // virtuals

    def contract(block, half):
        slab = domain[pl.ds(block * Q_BLOCK, Q_BLOCK)]
        stacked = slab.reshape(Q_BLOCK * virtuals, virtuals)
        for group in range(0, pairs, 2):
            product = jnp.dot(
                stacked,
                masked[:, group * virtuals : (group + 2) * virtuals],
                preferred_element_type=jnp.float32,
            ).astype(jnp.bfloat16)
            for pair in (group, group + 1):
                lane = (pair - group) * virtuals
                for q in range(Q_BLOCK):
                    half[
                        pair * virtuals : (pair + 1) * virtuals, q * virtuals : (q + 1) * virtuals
                    ] = product[q * virtuals : (q + 1) * virtuals, lane : lane + virtuals]

    def accumulate(block, half):
        slab = domain[pl.ds(block * Q_BLOCK, Q_BLOCK)]
        beside = jnp.concatenate([slab[q] for q in range(Q_BLOCK)], axis=1)
        total[...] += lax.dot_general(
            half[...], beside, ROWS_LAST, preferred_element_type=jnp.float32
        )

    buffers = (half_a, half_b)
    peeled = 1
    for i in range(peeled):
        if loaded is not None:
            loaded(first + i)
        contract(first + i, buffers[i % 2])
        if i > 0:
            accumulate(first + i - 1, buffers[(i - 1) % 2])
    if loaded is not None:
        for block in range(first + peeled, last):
            loaded(block)
    done, filled = first + peeled - 1, (peeled - 1) % 2
    held, spare = buffers[filled], buffers[1 - filled]

    @pl.loop(0, (last - 1 - done) // 2)
    def _(i):
        contract(done + 2 * i + 1, spare)
        accumulate(done + 2 * i, held)
        contract(done + 2 * i + 2, held)
        accumulate(done + 2 * i + 1, spare)

    if (last - 1 - done) % 2:
        contract(last - 1, spare)
        accumulate(last - 2, held)
        accumulate(last - 1, spare)
    else:
        accumulate(last - 1, held)


def split_rows(total, flipped, slabs, outs):
    virtuals = total.shape[1]
    pairs = total.shape[0] // virtuals
    per_side = math.isqrt(pairs)
    slab_rows, chips = virtuals // slabs, slabs // CORES
    vc_index = lax.axis_index("vc")
    core, chip = lax.rem(vc_index, CORES), vc_index // CORES
    for pair in range(pairs):
        at = slice(pair * virtuals, (pair + 1) * virtuals)
        flipped[at, :] = total[at, :].T
    for (core_step, chip_step, kind), out in outs.items():
        to_core = core if core_step == 0 else 1 - core
        start = (lax.rem(chip + chip_step, chips) * CORES + to_core) * slab_rows
        for pair in range(pairs):
            at = pl.ds(pl.multiple_of(pair * virtuals + start, slab_rows), slab_rows)
            if kind == 0:
                out[pair] = total[at, :]
            else:
                out[pair % per_side * per_side + pair // per_side] = flipped[at, :]


def places_of(core_step, array):
    return {
        (core_step, t, kind): array.at[t, kind] for t in range(array.shape[0]) for kind in range(2)
    }


def first_kernel(
    counts_in, amps_in, domain_in, keep, give, domain, masked_next,
    counts, amps, masked, total, flipped, half_a, half_b, small_sems, domain_sems,
):
    aux, virtuals = domain.shape[:2]
    per_side, row_slots = counts.shape
    halves = row_slots // per_side
    col_index = lax.axis_index("col")

    def domain_copy(block):
        rows = pl.ds(block * Q_BLOCK, Q_BLOCK)
        return pltpu.make_async_copy(domain_in.at[rows], domain.at[rows], domain_sems.at[block])

    def amps_copy(k):
        rows = pl.ds(lax.rem(col_index + k, halves) * per_side, per_side)
        return pltpu.make_async_copy(amps_in.at[rows], amps.at[k], small_sems.at[k])

    def mask(k, out):
        rows = lax.broadcasted_iota(jnp.int32, (virtuals, virtuals), 0)
        cols = lax.broadcasted_iota(jnp.int32, (virtuals, virtuals), 1)
        reach = jnp.maximum(rows, cols)
        half_index = lax.rem(col_index + k, halves)
        for pair in range(per_side * per_side):
            row_slot, col_slot = pair // per_side, pair % per_side
            tile = amps[k, row_slot, col_slot].astype(jnp.float32)
            limit = counts[col_slot, half_index * per_side + row_slot]
            kept = jnp.where(reach < limit, tile, 0.0)
            out[:, pair * virtuals : (pair + 1) * virtuals] = kept.astype(jnp.bfloat16)

    counts_copy = pltpu.make_async_copy(counts_in, counts, small_sems.at[halves])
    counts_copy.start()
    amps_copy(0).start()
    amps_copy(1).start()
    for block in range(aux // Q_BLOCK):
        domain_copy(block).start()
    total[...] = jnp.zeros_like(total)
    counts_copy.wait()
    amps_copy(0).wait()
    mask(0, masked)
    amps_copy(1).wait()
    mask(1, masked_next)
    add_blocks(
        0, aux // Q_BLOCK, domain, masked, total, half_a, half_b,
        lambda block: domain_copy(block).wait(),
    )
    split_rows(
        total, flipped, keep.shape[0] * CORES, {**places_of(0, keep), **places_of(1, give)}
    )


def opening_kernel(last, masked, domain, total, half_a, half_b):
    total[...] = jnp.zeros_like(total)
    add_blocks(0, last, domain, masked, total, half_a, half_b)


def closing_kernel(
    first, masked, total_in, domain, keep, give, give_first, total, flipped, half_a, half_b
):
    chips = keep.shape[0]
    total[...] = total_in[...]
    blocks = domain.shape[0] // Q_BLOCK
    add_blocks(first, blocks, domain, masked, total, half_a, half_b)
    outs = places_of(0, keep)
    for t in range(chips):
        outs[1, t, 0] = give.at[t]
    outs[1, 0, 1] = give.at[chips]
    for t in range(1, chips):
        outs[1, t, 1] = give_first.at[t - 1]
    split_rows(total, flipped, chips * CORES, outs)


def ladder_calls(slabs, counts, amps, domain):
    aux, virtuals = domain.shape[:2]
    per_side, row_slots = counts.shape
    pairs = per_side * per_side
    chips = slabs // CORES

    def rows_of(*ahead):
        return jax.ShapeDtypeStruct((*ahead, pairs, virtuals // slabs, virtuals), jnp.float32)

    made = rows_of(chips, 2)
    masked = jax.ShapeDtypeStruct((virtuals, pairs * virtuals), jnp.bfloat16)
    total = jax.ShapeDtypeStruct((pairs * virtuals, virtuals), jnp.float32)
    half = jax.ShapeDtypeStruct((pairs * virtuals, Q_BLOCK * virtuals), jnp.bfloat16)
    vmem = pl.BlockSpec(memory_space=pltpu.VMEM)
    hbm = pl.BlockSpec(memory_space=pltpu.HBM)

    def call(kernel, name, span, in_specs, outs, scratch, more_scratch=()):
        return pl.pallas_call(
            kernel,
            in_specs=in_specs,
            out_specs=[vmem] * len(outs),
            out_shape=outs,
            scratch_shapes=[pltpu.VMEM(x.shape, x.dtype) for x in scratch] + list(more_scratch),
            compiler_params=pltpu.CompilerParams(vmem_limit_bytes=32 * 2**20),
            cost_estimate=pl.CostEstimate(
                flops=4 * pairs * span * Q_BLOCK * virtuals**3,
                bytes_accessed=2 * span * Q_BLOCK * virtuals**2,
                transcendentals=0,
            ),
            name=name,
        )

    def first_half():
        operands = [pltpu.with_memory_space_constraint(x, pltpu.HBM) for x in (counts, amps, domain)]

        def kernel(*refs):
            *arrays, counts_here, small_sems, domain_sems = refs
            first_kernel(*arrays[:7], counts_here, *arrays[7:], small_sems, domain_sems)

        return call(
            kernel,
            "first_half",
            aux // Q_BLOCK,
            [hbm] * 3,
            [made, made, jax.ShapeDtypeStruct(domain.shape, domain.dtype), masked],
            [
                jax.ShapeDtypeStruct((row_slots // per_side, per_side, *amps.shape[1:]), amps.dtype),
                masked, total, total, half, half,
            ],
            [
                pltpu.SMEM(counts.shape, counts.dtype),
                pltpu.SemaphoreType.DMA((row_slots // per_side + 1,)),
                pltpu.SemaphoreType.DMA((aux // Q_BLOCK,)),
            ],
        )(*operands)

    def second_opens(last, masked_1, domain):
        return call(
            functools.partial(opening_kernel, last), "second_opens", last, [vmem] * 2, [total], [half, half]
        )(masked_1, domain)[0]

    def second_closes(first, masked_1, total_1, domain):
        return call(
            functools.partial(closing_kernel, first),
            "second_closes",
            aux // Q_BLOCK - first,
            [vmem] * 3,
            [made, rows_of(chips + 1), rows_of(chips - 1)],
            [total, total, half, half],
        )(masked_1, total_1, domain)

    return first_half, second_opens, second_closes


def on_device(rows, cols, slabs, amplitudes, factors, pno_counts, pair_live):
    row_slots, per_side = amplitudes.shape[:2]
    halves = row_slots // per_side
    slab_rows, virtuals = amplitudes.shape[2] // slabs, amplitudes.shape[2]
    domain = factors[0, 0]
    row_index, col_index, vc_index = (lax.axis_index(name) for name in AXES)
    reach = jnp.maximum(
        vc_index * slab_rows + lax.broadcasted_iota(jnp.int32, (slab_rows, virtuals), 0),
        lax.broadcasted_iota(jnp.int32, (slab_rows, virtuals), 1),
    )
    limits = jnp.where(pair_live > 0, pno_counts, 0)
    kept_cells = lax.optimization_barrier(
        (reach[None, None] < limits[:, :, None, None]).astype(jnp.float32)
    )

    def send(array, target):
        places = [(r, c, v) for r in range(rows) for c in range(cols) for v in range(slabs)]

        def flat(r, c, v):
            return (r * cols + c) * slabs + v

        return lax.ppermute(array, AXES, [(flat(*place), flat(*target(*place))) for place in places])

    def to_chips(given):
        return [
            send(part, lambda r, c, v, t=t: (r, c, (v + t * CORES) % slabs))
            for t, part in enumerate(given, 1)
        ]

    def mirror_of(k, r, c):
        return c // halves, r * halves + (c + k) % halves

    def to_mirror(k, flipped):
        def target(r, c, v):
            return (r, c, v ^ 1) if mirror_of(k, r, c) == (r, c) else (*mirror_of(k, r, c), v)

        got = send(flipped, target)
        if not any(mirror_of(k, r, c) == (r, c) for r in range(rows) for c in range(cols)):
            return got
        at_row, at_col = mirror_of(k, row_index, col_index)
        return jnp.where((at_row == row_index) & (at_col == col_index), flipped, got)

    def sum_of(*parts):
        return functools.reduce(jnp.add, parts)

    tie = lax.optimization_barrier
    opening, chips = 1, slabs // CORES
    assert halves == 2
    first_half, second_opens, second_closes = ladder_calls(slabs, pno_counts.T, amplitudes, domain)

    def to_core(give):
        return send(give, lambda r, c, v: (r, c, v ^ 1))

    keep_0, give_0, domain, masked_1 = first_half()
    got_0 = to_core(give_0)
    opened = second_opens(opening, masked_1, domain)
    got_0, opened = tie((got_0, opened))
    parts_0 = to_chips([keep_0[t] + got_0[t] for t in range(1, chips)])
    keep_1, give_1, give_first = second_closes(opening, masked_1, opened, domain)
    give_1, give_first, parts_0 = tie((give_1, give_first, parts_0))
    flipped_0 = sum_of(keep_0[0, 1], got_0[0, 1], *[part[1] for part in parts_0])
    mirror_0 = to_mirror(0, flipped_0)
    got_first = to_core(give_first)
    given = [keep_1[t, 1] + got_first[t - 1] for t in range(1, chips)]
    flips = to_chips(given)
    got_1 = to_core(tie((give_1, given))[0])
    flipped_1 = sum_of(keep_1[0, 1], got_1[chips], *flips)
    given = [keep_1[t, 0] + got_1[t] for t in range(1, chips)]
    flipped_1, given = tie((flipped_1, given))
    mirror_1 = to_mirror(1, flipped_1)
    owns = to_chips(given)
    done = [
        sum_of(keep_0[0, 0], got_0[0, 0], *[part[0] for part in parts_0], mirror_0),
        sum_of(keep_1[0, 0], got_1[0], mirror_1, *owns),
    ]
    done = [x.reshape(per_side, per_side, slab_rows, virtuals) for x in done]
    turn = lax.rem(col_index, halves)
    ordered = []
    for half in range(halves):
        value = done[half]
        for other in range(1, halves):
            value = jnp.where(turn == other, done[(half - other) % halves], value)
        ordered.append(value)
    return jnp.where(kept_cells > 0, jnp.concatenate(ordered), 0.0)


def solution(mesh):
    in_specs = (
        P("row", "col", None, None),
        P("row", "col", "vc", None, None),
        P("row", "col"),
        P("row", "col"),
    )
    body = functools.partial(on_device, *(mesh.shape[name] for name in AXES))
    return jax.shard_map(
        body, mesh=mesh, in_specs=in_specs, out_specs=P("row", "col", "vc", None), check_vma=False
    )
```

```python
import functools

import jax
import jax.numpy as jnp
from jax import lax
from jax.experimental import pallas as pl
from jax.experimental.pallas import tpu as pltpu
from jax.sharding import PartitionSpec as P

AXES = ("row", "col", "vc")
CORES = 2
Q_BLOCK = 8
ROWS_LAST = (((1,), (1,)), ((), ()))


def add_blocks(first, last, domain, masked, total, half_a, half_b, rows=None, loaded=None, unroll=False):
    virtuals = domain.shape[1]
    pairs = total.shape[0] // virtuals
    size = half_a.shape[1] // virtuals
    rows = rows or (virtuals,) * (pairs // 2)
    places, end = [], 0
    for pair in range(pairs):
        places.append((pair, end, rows[pair // 2]))
        end += rows[pair // 2]

    def contract(block, half):
        for group, height in enumerate(rows):
            if height == 0:
                continue
            stacked = domain[pl.ds(block * size, size), :height].reshape(size * height, virtuals)
            product = jnp.dot(
                stacked,
                masked[:, 2 * group * virtuals : 2 * (group + 1) * virtuals],
                preferred_element_type=jnp.float32,
            ).astype(jnp.bfloat16)
            for pair, start, _ in places[2 * group : 2 * (group + 1)]:
                lane = (pair - 2 * group) * virtuals
                for q in range(size):
                    half[start : start + height, q * virtuals : (q + 1) * virtuals] = product[
                        q * height : (q + 1) * height, lane : lane + virtuals
                    ]

    def accumulate(block, half):
        slab = domain[pl.ds(block * size, size)]
        beside = jnp.concatenate([slab[q] for q in range(size)], axis=1)
        added = lax.dot_general(
            half[:end], beside, ROWS_LAST, preferred_element_type=jnp.float32
        )
        for pair, start, height in places:
            if height > 0:
                total[pair * virtuals : pair * virtuals + height] += added[start : start + height]

    loaded = loaded or (lambda block: None)
    contract(first, half_a)

    @pl.loop(0, (last - 1 - first) // 2, unroll=unroll)
    def _(i):
        loaded(first + 2 * i + 1)
        loaded(first + 2 * i + 2)
        contract(first + 2 * i + 1, half_b)
        accumulate(first + 2 * i, half_a)
        contract(first + 2 * i + 2, half_a)
        accumulate(first + 2 * i + 1, half_b)

    if (last - 1 - first) % 2:
        loaded(last - 1)
        contract(last - 1, half_b)
        accumulate(last - 2, half_a)
        accumulate(last - 1, half_b)
    else:
        accumulate(last - 1, half_a)


def sides_of(pair, pairs):
    bits = (pairs.bit_length() - 1) // 2
    return pair >> bits, pair & ((1 << bits) - 1)


def mirror_place(pair, pairs):
    row, col = sides_of(pair, pairs)
    return (col << ((pairs.bit_length() - 1) // 2)) | row


def split_rows(total, flipped, slabs, outs, order=None):
    virtuals = total.shape[1]
    pairs = total.shape[0] // virtuals
    order = order or range(pairs)
    mirrors = [mirror_place(pair, pairs) for pair in order]
    slab_rows, chips = virtuals // slabs, slabs // CORES
    vc_index = lax.axis_index("vc")
    core, chip = lax.rem(vc_index, CORES), vc_index // CORES
    for pair in range(pairs):
        at = slice(pair * virtuals, (pair + 1) * virtuals)
        flipped[at, :] = total[at, :].T
    for (core_step, chip_step, kind), out in outs.items():
        to_core = core if core_step == 0 else 1 - core
        start = (lax.rem(chip + chip_step, chips) * CORES + to_core) * slab_rows
        for tile, (pair, mirror) in enumerate(zip(order, mirrors)):
            at = pl.ds(pl.multiple_of(tile * virtuals + start, slab_rows), slab_rows)
            if kind == 0:
                out[pair] = total[at, :]
            else:
                out[mirror] = flipped[at, :]


def places_of(core_step, array):
    return {
        (core_step, t, kind): array.at[t, kind] for t in range(array.shape[0]) for kind in range(2)
    }


def first_kernel(
    counts_in, live_in, amps_in, domain_in, keep, give, domain, masked_next,
    counts, live, amps, masked, total, flipped, half_a, half_b, small_sems, domain_sems,
):
    aux, virtuals = domain.shape[:2]
    per_side, row_slots = counts.shape
    pairs = per_side * per_side
    halves = row_slots // per_side
    blocks = aux // Q_BLOCK
    col_index = lax.axis_index("col")

    def domain_copy(block):
        rows = pl.ds(block * Q_BLOCK, Q_BLOCK)
        return pltpu.make_async_copy(domain_in.at[rows], domain.at[rows], domain_sems.at[block])

    def amps_copy(k):
        rows = pl.ds(lax.rem(col_index + k, halves) * per_side, per_side)
        return pltpu.make_async_copy(amps_in.at[rows], amps.at[k], small_sems.at[k])

    def limit(k, pair):
        slot = lax.rem(col_index + k, halves) * per_side + pair // per_side
        return jnp.where(live[pair % per_side, slot] > 0, counts[pair % per_side, slot], 0)

    def mask(k, out, limits, order):
        rows = lax.broadcasted_iota(jnp.int32, (virtuals, virtuals), 0)
        cols = lax.broadcasted_iota(jnp.int32, (virtuals, virtuals), 1)
        reach = jnp.maximum(rows, cols)
        for tile, pair in enumerate(order):
            amp = amps[k, *sides_of(pair, pairs)].astype(jnp.float32)
            kept = jnp.where(reach < limits[tile], amp, 0.0)
            out[:, tile * virtuals : (tile + 1) * virtuals] = kept.astype(jnp.bfloat16)

    copies = [
        pltpu.make_async_copy(counts_in, counts, small_sems.at[halves]),
        pltpu.make_async_copy(live_in, live, small_sems.at[halves + 1]),
        *[amps_copy(k) for k in range(halves)],
    ]
    for copy in copies:
        copy.start()
    for block in range(blocks):
        domain_copy(block).start()
    total[...] = jnp.zeros_like(total)
    for copy in copies:
        copy.wait()
    keys = [limit(0, pair) * pairs + pair for pair in range(pairs)]
    for done in range(pairs - 1):
        for i in range(pairs - 1 - done):
            keys[i : i + 2] = jnp.maximum(*keys[i : i + 2]), jnp.minimum(*keys[i : i + 2])
    limits = [key >> (pairs.bit_length() - 1) for key in keys]
    order = [key & (pairs - 1) for key in keys]
    mask(0, masked, limits, order)
    mask(1, masked_next, [limit(1, pair) for pair in range(pairs)], range(pairs))
    domain_copy(0).wait()

    levels = [0, virtuals // 2, 3 * virtuals // 4, virtuals]
    reached = [sum((x > bound).astype(jnp.int32) for bound in levels[:-1]) for x in limits[::2]]
    for high in range(len(levels)):
        for low in range(high + 1):
            @pl.when((reached[0] == high) & (reached[1] == low))
            def _(rows=(levels[high], levels[low])):
                if rows[0] == 0:
                    for block in range(1, blocks):
                        domain_copy(block).wait()
                else:
                    add_blocks(
                        0, blocks, domain, masked, total, half_a, half_b, rows,
                        lambda block: domain_copy(block).wait(),
                    )

    split_rows(
        total, flipped, keep.shape[0] * CORES, {**places_of(0, keep), **places_of(1, give)}, order
    )


def opening_kernel(masked, domain, total, half):
    total[...] = jnp.zeros_like(total)
    add_blocks(0, 1, domain, masked, total, half, half)


def closing_kernel(
    first, masked, total_in, domain, keep, give, give_first, total, flipped, half_a, half_b
):
    chips = keep.shape[0]
    total[...] = total_in[...]
    blocks = domain.shape[0] // Q_BLOCK
    add_blocks(first, blocks, domain, masked, total, half_a, half_b, unroll=True)
    outs = places_of(0, keep)
    for t in range(chips):
        outs[1, t, 0] = give.at[t]
    outs[1, 0, 1] = give.at[chips]
    for t in range(1, chips):
        outs[1, t, 1] = give_first.at[t - 1]
    split_rows(total, flipped, chips * CORES, outs)


def ladder_calls(slabs, counts, live, amps, domain):
    aux, virtuals = domain.shape[:2]
    per_side, row_slots = counts.shape
    pairs = per_side * per_side
    chips = slabs // CORES

    def rows_of(*ahead):
        return jax.ShapeDtypeStruct((*ahead, pairs, virtuals // slabs, virtuals), jnp.float32)

    made = rows_of(chips, 2)
    masked = jax.ShapeDtypeStruct((virtuals, pairs * virtuals), jnp.bfloat16)
    total = jax.ShapeDtypeStruct((pairs * virtuals, virtuals), jnp.float32)

    def half_of(size):
        return jax.ShapeDtypeStruct((pairs * virtuals, size * virtuals), jnp.bfloat16)

    half = half_of(Q_BLOCK)
    vmem = pl.BlockSpec(memory_space=pltpu.VMEM)
    hbm = pl.BlockSpec(memory_space=pltpu.HBM)

    def call(kernel, name, span, in_specs, outs, scratch, more_scratch=()):
        return pl.pallas_call(
            kernel,
            in_specs=in_specs,
            out_specs=[vmem] * len(outs),
            out_shape=outs,
            scratch_shapes=[pltpu.VMEM(x.shape, x.dtype) for x in scratch] + list(more_scratch),
            compiler_params=pltpu.CompilerParams(vmem_limit_bytes=32 * 2**20),
            cost_estimate=pl.CostEstimate(
                flops=4 * pairs * span * Q_BLOCK * virtuals**3,
                bytes_accessed=2 * span * Q_BLOCK * virtuals**2,
                transcendentals=0,
            ),
            name=name,
        )

    def first_half():
        operands = [pltpu.with_memory_space_constraint(x, pltpu.HBM) for x in (counts, live, amps, domain)]

        def kernel(*refs):
            *arrays, counts_here, live_here, small_sems, domain_sems = refs
            first_kernel(*arrays[:8], counts_here, live_here, *arrays[8:], small_sems, domain_sems)

        return call(
            kernel,
            "first_half",
            aux // Q_BLOCK,
            [hbm] * 4,
            [made, made, jax.ShapeDtypeStruct(domain.shape, domain.dtype), masked],
            [
                jax.ShapeDtypeStruct((row_slots // per_side, per_side, *amps.shape[1:]), amps.dtype),
                masked, total, total, half, half,
            ],
            [
                pltpu.SMEM(counts.shape, counts.dtype),
                pltpu.SMEM(live.shape, live.dtype),
                pltpu.SemaphoreType.DMA((row_slots // per_side + 2,)),
                pltpu.SemaphoreType.DMA((aux // Q_BLOCK,)),
            ],
        )(*operands)

    def second_opens(last, masked_1, domain):
        return call(
            opening_kernel, "second_opens", last, [vmem] * 2, [total], [half_of(last * Q_BLOCK)]
        )(masked_1, domain)[0]

    def second_closes(first, masked_1, total_1, domain):
        return call(
            functools.partial(closing_kernel, first),
            "second_closes",
            aux // Q_BLOCK - first,
            [vmem] * 3,
            [made, rows_of(chips + 1), rows_of(chips - 1)],
            [total, total, half, half],
        )(masked_1, total_1, domain)

    return first_half, second_opens, second_closes


def on_device(rows, cols, slabs, amplitudes, factors, pno_counts, pair_live):
    row_slots, per_side = amplitudes.shape[:2]
    halves = row_slots // per_side
    slab_rows, virtuals = amplitudes.shape[2] // slabs, amplitudes.shape[2]
    domain = factors[0, 0]
    row_index, col_index, vc_index = (lax.axis_index(name) for name in AXES)
    reach = jnp.maximum(
        vc_index * slab_rows + lax.broadcasted_iota(jnp.int32, (slab_rows, virtuals), 0),
        lax.broadcasted_iota(jnp.int32, (slab_rows, virtuals), 1),
    )
    limits = jnp.where(pair_live > 0, pno_counts, 0)
    kept_cells = lax.optimization_barrier(
        (reach[None, None] < limits[:, :, None, None]).astype(jnp.float32)
    )

    def send(array, target):
        places = [(r, c, v) for r in range(rows) for c in range(cols) for v in range(slabs)]

        def flat(r, c, v):
            return (r * cols + c) * slabs + v

        return lax.ppermute(array, AXES, [(flat(*place), flat(*target(*place))) for place in places])

    def to_chips(given):
        return [
            send(part, lambda r, c, v, t=t: (r, c, (v + t * CORES) % slabs))
            for t, part in enumerate(given, 1)
        ]

    def mirror_of(k, r, c):
        return c // halves, r * halves + (c + k) % halves

    def to_mirror(k, flipped):
        def target(r, c, v):
            return (r, c, v ^ 1) if mirror_of(k, r, c) == (r, c) else (*mirror_of(k, r, c), v)

        got = send(flipped, target)
        if not any(mirror_of(k, r, c) == (r, c) for r in range(rows) for c in range(cols)):
            return got
        at_row, at_col = mirror_of(k, row_index, col_index)
        return jnp.where((at_row == row_index) & (at_col == col_index), flipped, got)

    def sum_of(*parts):
        return functools.reduce(jnp.add, parts)

    tie = lax.optimization_barrier
    opening, chips = 2, slabs // CORES
    assert halves == 2
    first_half, second_opens, second_closes = ladder_calls(slabs, pno_counts.T, pair_live.T, amplitudes, domain)

    def to_core(give):
        return send(give, lambda r, c, v: (r, c, v ^ 1))

    keep_0, give_0, domain, masked_1 = first_half()
    got_0 = to_core(give_0)
    opened = second_opens(opening, masked_1, domain)
    got_0, opened = tie((got_0, opened))
    parts_0 = to_chips([keep_0[t] + got_0[t] for t in range(1, chips)])
    keep_1, give_1, give_first = second_closes(opening, masked_1, opened, domain)
    give_1, give_first, parts_0 = tie((give_1, give_first, parts_0))
    flipped_0 = sum_of(keep_0[0, 1], got_0[0, 1], *[part[1] for part in parts_0])
    mirror_0 = to_mirror(0, flipped_0)
    got_first = to_core(give_first)
    given = [keep_1[t, 1] + got_first[t - 1] for t in range(1, chips)]
    flips = to_chips(given)
    got_1 = to_core(tie((give_1, given))[0])
    flipped_1 = sum_of(keep_1[0, 1], got_1[chips], *flips)
    given = [keep_1[t, 0] + got_1[t] for t in range(1, chips)]
    flipped_1, given = tie((flipped_1, given))
    mirror_1 = to_mirror(1, flipped_1)
    owns = to_chips(given)
    done = [
        sum_of(keep_0[0, 0], got_0[0, 0], *[part[0] for part in parts_0], mirror_0),
        sum_of(keep_1[0, 0], got_1[0], mirror_1, *owns),
    ]
    done = [x.reshape(per_side, per_side, slab_rows, virtuals) for x in done]
    turn = lax.rem(col_index, halves)
    ordered = []
    for half in range(halves):
        value = done[half]
        for other in range(1, halves):
            value = jnp.where(turn == other, done[(half - other) % halves], value)
        ordered.append(value)
    return jnp.where(kept_cells > 0, jnp.concatenate(ordered), 0.0)


def solution(mesh):
    in_specs = (
        P("row", "col", None, None),
        P("row", "col", "vc", None, None),
        P("row", "col"),
        P("row", "col"),
    )
    body = functools.partial(on_device, *(mesh.shape[name] for name in AXES))
    return jax.shard_map(
        body, mesh=mesh, in_specs=in_specs, out_specs=P("row", "col", "vc", None), check_vma=False
    )
```

```python
import functools

import jax
import jax.numpy as jnp
from jax import lax
from jax.experimental import pallas as pl
from jax.experimental.pallas import tpu as pltpu
from jax.sharding import PartitionSpec as P

AXES = ("row", "col", "vc")
CORES = 2
Q_BLOCK = 8
ROWS_LAST = (((1,), (1,)), ((), ()))


def add_blocks(first, last, domain, masked, total, half_a, half_b, rows=None, loaded=None, unroll=False):
    virtuals = domain.shape[1]
    pairs = total.shape[0] // virtuals
    size = half_a.shape[1] // virtuals
    rows = rows or (virtuals,) * (pairs // 2)
    places, end = [], 0
    for pair in range(pairs):
        places.append((pair, end, rows[pair // 2]))
        end += rows[pair // 2]

    def contract(block, half):
        for group, height in enumerate(rows):
            if height == 0:
                continue
            stacked = domain[pl.ds(block * size, size), :height].reshape(size * height, virtuals)
            product = jnp.dot(
                stacked,
                masked[:, 2 * group * virtuals : 2 * (group + 1) * virtuals],
                preferred_element_type=jnp.float32,
            ).astype(jnp.bfloat16)
            for pair, start, _ in places[2 * group : 2 * (group + 1)]:
                lane = (pair - 2 * group) * virtuals
                for q in range(size):
                    half[start : start + height, q * virtuals : (q + 1) * virtuals] = product[
                        q * height : (q + 1) * height, lane : lane + virtuals
                    ]

    def accumulate(block, half):
        slab = domain[pl.ds(block * size, size)]
        beside = jnp.concatenate([slab[q] for q in range(size)], axis=1)
        added = lax.dot_general(
            half[:end], beside, ROWS_LAST, preferred_element_type=jnp.float32
        )
        for pair, start, height in places:
            if height > 0:
                total[pair * virtuals : pair * virtuals + height] += added[start : start + height]

    loaded = loaded or (lambda block: None)
    contract(first, half_a)

    @pl.loop(0, (last - 1 - first) // 2, unroll=unroll)
    def _(i):
        loaded(first + 2 * i + 1)
        loaded(first + 2 * i + 2)
        contract(first + 2 * i + 1, half_b)
        accumulate(first + 2 * i, half_a)
        contract(first + 2 * i + 2, half_a)
        accumulate(first + 2 * i + 1, half_b)

    if (last - 1 - first) % 2:
        loaded(last - 1)
        contract(last - 1, half_b)
        accumulate(last - 2, half_a)
        accumulate(last - 1, half_b)
    else:
        accumulate(last - 1, half_a)


def sides_of(pair, pairs):
    bits = (pairs.bit_length() - 1) // 2
    return pair >> bits, pair & ((1 << bits) - 1)


def mirror_place(pair, pairs):
    row, col = sides_of(pair, pairs)
    return (col << ((pairs.bit_length() - 1) // 2)) | row


def split_rows(total, flipped, slabs, outs, order=None):
    virtuals = total.shape[1]
    pairs = total.shape[0] // virtuals
    order = order or range(pairs)
    mirrors = [mirror_place(pair, pairs) for pair in order]
    slab_rows, chips = virtuals // slabs, slabs // CORES
    vc_index = lax.axis_index("vc")
    core, chip = lax.rem(vc_index, CORES), vc_index // CORES
    for pair in range(pairs):
        at = slice(pair * virtuals, (pair + 1) * virtuals)
        flipped[at, :] = total[at, :].T
    for (core_step, chip_step, kind), out in outs.items():
        to_core = core if core_step == 0 else 1 - core
        start = (lax.rem(chip + chip_step, chips) * CORES + to_core) * slab_rows
        for tile, (pair, mirror) in enumerate(zip(order, mirrors)):
            at = pl.ds(pl.multiple_of(tile * virtuals + start, slab_rows), slab_rows)
            if kind == 0:
                out[pair] = total[at, :]
            else:
                out[mirror] = flipped[at, :]


def places_of(core_step, array):
    return {
        (core_step, t, kind): array.at[t, kind] for t in range(array.shape[0]) for kind in range(2)
    }


def first_kernel(
    counts_in, live_in, amps_in, domain_in, keep, give, domain, masked_next,
    counts, live, amps, masked, total, flipped, half_a, half_b, small_sems, domain_sems,
):
    aux, virtuals = domain.shape[:2]
    per_side, row_slots = counts.shape
    pairs = per_side * per_side
    halves = row_slots // per_side
    blocks = aux // Q_BLOCK
    col_index = lax.axis_index("col")

    def domain_copy(block):
        rows = pl.ds(block * Q_BLOCK, Q_BLOCK)
        return pltpu.make_async_copy(domain_in.at[rows], domain.at[rows], domain_sems.at[block])

    def amps_copy(k):
        rows = pl.ds(lax.rem(col_index + 1 + k, halves) * per_side, per_side)
        return pltpu.make_async_copy(amps_in.at[rows], amps.at[k], small_sems.at[k])

    def limit(k, pair):
        slot = lax.rem(col_index + 1 + k, halves) * per_side + pair // per_side
        return jnp.where(live[pair % per_side, slot] > 0, counts[pair % per_side, slot], 0)

    def mask(k, out, limits, order):
        rows = lax.broadcasted_iota(jnp.int32, (virtuals, virtuals), 0)
        cols = lax.broadcasted_iota(jnp.int32, (virtuals, virtuals), 1)
        reach = jnp.maximum(rows, cols)
        for tile, pair in enumerate(order):
            amp = amps[k, *sides_of(pair, pairs)].astype(jnp.float32)
            kept = jnp.where(reach < limits[tile], amp, 0.0)
            out[:, tile * virtuals : (tile + 1) * virtuals] = kept.astype(jnp.bfloat16)

    copies = [
        pltpu.make_async_copy(counts_in, counts, small_sems.at[halves]),
        pltpu.make_async_copy(live_in, live, small_sems.at[halves + 1]),
        *[amps_copy(k) for k in range(halves)],
    ]
    for copy in copies:
        copy.start()
    for block in range(blocks):
        domain_copy(block).start()
    total[...] = jnp.zeros_like(total)
    for copy in copies:
        copy.wait()
    keys = [limit(0, pair) * pairs + pair for pair in range(pairs)]
    for done in range(pairs - 1):
        for i in range(pairs - 1 - done):
            keys[i : i + 2] = jnp.maximum(*keys[i : i + 2]), jnp.minimum(*keys[i : i + 2])
    limits = [key >> (pairs.bit_length() - 1) for key in keys]
    order = [key & (pairs - 1) for key in keys]
    mask(0, masked, limits, order)
    mask(1, masked_next, [limit(1, pair) for pair in range(pairs)], range(pairs))
    domain_copy(0).wait()

    levels = [0, virtuals // 2, 3 * virtuals // 4, virtuals]
    reached = [sum((x > bound).astype(jnp.int32) for bound in levels[:-1]) for x in limits[::2]]
    for high in range(len(levels)):
        for low in range(high + 1):
            @pl.when((reached[0] == high) & (reached[1] == low))
            def _(rows=(levels[high], levels[low])):
                if rows[0] == 0:
                    for block in range(1, blocks):
                        domain_copy(block).wait()
                else:
                    add_blocks(
                        0, blocks, domain, masked, total, half_a, half_b, rows,
                        lambda block: domain_copy(block).wait(),
                    )

    split_rows(
        total, flipped, keep.shape[0] * CORES, {**places_of(0, keep), **places_of(1, give)}, order
    )


def opening_kernel(masked, domain, total, half):
    total[...] = jnp.zeros_like(total)
    add_blocks(0, 1, domain, masked, total, half, half)


def closing_kernel(
    first, masked, total_in, domain, keep, give, give_first, total, flipped, half_a, half_b
):
    chips = keep.shape[0]
    total[...] = total_in[...]
    blocks = domain.shape[0] // Q_BLOCK
    add_blocks(first, blocks, domain, masked, total, half_a, half_b, unroll=True)
    outs = places_of(0, keep)
    for t in range(chips):
        outs[1, t, 0] = give.at[t]
    outs[1, 0, 1] = give.at[chips]
    for t in range(1, chips):
        outs[1, t, 1] = give_first.at[t - 1]
    split_rows(total, flipped, chips * CORES, outs)


def ladder_calls(slabs, counts, live, amps, domain):
    aux, virtuals = domain.shape[:2]
    per_side, row_slots = counts.shape
    pairs = per_side * per_side
    chips = slabs // CORES

    def rows_of(*ahead):
        return jax.ShapeDtypeStruct((*ahead, pairs, virtuals // slabs, virtuals), jnp.float32)

    made = rows_of(chips, 2)
    masked = jax.ShapeDtypeStruct((virtuals, pairs * virtuals), jnp.bfloat16)
    total = jax.ShapeDtypeStruct((pairs * virtuals, virtuals), jnp.float32)

    def half_of(size):
        return jax.ShapeDtypeStruct((pairs * virtuals, size * virtuals), jnp.bfloat16)

    half = half_of(Q_BLOCK)
    vmem = pl.BlockSpec(memory_space=pltpu.VMEM)
    hbm = pl.BlockSpec(memory_space=pltpu.HBM)

    def call(kernel, name, span, in_specs, outs, scratch, more_scratch=()):
        return pl.pallas_call(
            kernel,
            in_specs=in_specs,
            out_specs=[vmem] * len(outs),
            out_shape=outs,
            scratch_shapes=[pltpu.VMEM(x.shape, x.dtype) for x in scratch] + list(more_scratch),
            compiler_params=pltpu.CompilerParams(vmem_limit_bytes=32 * 2**20),
            cost_estimate=pl.CostEstimate(
                flops=4 * pairs * span * Q_BLOCK * virtuals**3,
                bytes_accessed=2 * span * Q_BLOCK * virtuals**2,
                transcendentals=0,
            ),
            name=name,
        )

    def first_half():
        operands = [pltpu.with_memory_space_constraint(x, pltpu.HBM) for x in (counts, live, amps, domain)]

        def kernel(*refs):
            *arrays, counts_here, live_here, small_sems, domain_sems = refs
            first_kernel(*arrays[:8], counts_here, live_here, *arrays[8:], small_sems, domain_sems)

        return call(
            kernel,
            "first_half",
            aux // Q_BLOCK,
            [hbm] * 4,
            [made, made, jax.ShapeDtypeStruct(domain.shape, domain.dtype), masked],
            [
                jax.ShapeDtypeStruct((row_slots // per_side, per_side, *amps.shape[1:]), amps.dtype),
                masked, total, total, half, half,
            ],
            [
                pltpu.SMEM(counts.shape, counts.dtype),
                pltpu.SMEM(live.shape, live.dtype),
                pltpu.SemaphoreType.DMA((row_slots // per_side + 2,)),
                pltpu.SemaphoreType.DMA((aux // Q_BLOCK,)),
            ],
        )(*operands)

    def second_opens(last, masked_1, domain):
        return call(
            opening_kernel, "second_opens", last, [vmem] * 2, [total], [half_of(last * Q_BLOCK)]
        )(masked_1, domain)[0]

    def second_closes(first, masked_1, total_1, domain):
        return call(
            functools.partial(closing_kernel, first),
            "second_closes",
            aux // Q_BLOCK - first,
            [vmem] * 3,
            [made, rows_of(chips + 1), rows_of(chips - 1)],
            [total, total, half, half],
        )(masked_1, total_1, domain)

    return first_half, second_opens, second_closes


def on_device(rows, cols, slabs, amplitudes, factors, pno_counts, pair_live):
    row_slots, per_side = amplitudes.shape[:2]
    halves = row_slots // per_side
    slab_rows, virtuals = amplitudes.shape[2] // slabs, amplitudes.shape[2]
    domain = factors[0, 0]
    row_index, col_index, vc_index = (lax.axis_index(name) for name in AXES)
    reach = jnp.maximum(
        vc_index * slab_rows + lax.broadcasted_iota(jnp.int32, (slab_rows, virtuals), 0),
        lax.broadcasted_iota(jnp.int32, (slab_rows, virtuals), 1),
    )
    limits = jnp.where(pair_live > 0, pno_counts, 0)
    kept_cells = lax.optimization_barrier(
        (reach[None, None] < limits[:, :, None, None]).astype(jnp.float32)
    )

    def send(array, target):
        places = [(r, c, v) for r in range(rows) for c in range(cols) for v in range(slabs)]

        def flat(r, c, v):
            return (r * cols + c) * slabs + v

        return lax.ppermute(array, AXES, [(flat(*place), flat(*target(*place))) for place in places])

    def to_chips(given):
        return [
            send(part, lambda r, c, v, t=t: (r, c, (v + t * CORES) % slabs))
            for t, part in enumerate(given, 1)
        ]

    def mirror_of(k, r, c):
        return c // halves, r * halves + (c + 1 + k) % halves

    def to_mirror(k, flipped):
        def target(r, c, v):
            return (r, c, v ^ 1) if mirror_of(k, r, c) == (r, c) else (*mirror_of(k, r, c), v)

        got = send(flipped, target)
        if not any(mirror_of(k, r, c) == (r, c) for r in range(rows) for c in range(cols)):
            return got
        at_row, at_col = mirror_of(k, row_index, col_index)
        return jnp.where((at_row == row_index) & (at_col == col_index), flipped, got)

    def sum_of(*parts):
        return functools.reduce(jnp.add, parts)

    tie = lax.optimization_barrier
    opening, chips = 2, slabs // CORES
    assert halves == 2
    first_half, second_opens, second_closes = ladder_calls(slabs, pno_counts.T, pair_live.T, amplitudes, domain)

    def to_core(give):
        return send(give, lambda r, c, v: (r, c, v ^ 1))

    keep_0, give_0, domain, masked_1 = first_half()
    got_0 = to_core(give_0)
    opened = second_opens(opening, masked_1, domain)
    got_0, opened = tie((got_0, opened))
    parts_0 = to_chips([keep_0[t] + got_0[t] for t in range(1, chips)])
    keep_1, give_1, give_first = second_closes(opening, masked_1, opened, domain)
    give_1, give_first, parts_0 = tie((give_1, give_first, parts_0))
    flipped_0 = sum_of(keep_0[0, 1], got_0[0, 1], *[part[1] for part in parts_0])
    mirror_0 = to_mirror(0, flipped_0)
    got_first = to_core(give_first)
    given = [keep_1[t, 1] + got_first[t - 1] for t in range(1, chips)]
    flips = to_chips(given)
    got_1 = to_core(tie((give_1, given))[0])
    flipped_1 = sum_of(keep_1[0, 1], got_1[chips], *flips)
    given = [keep_1[t, 0] + got_1[t] for t in range(1, chips)]
    flipped_1, given = tie((flipped_1, given))
    mirror_1 = to_mirror(1, flipped_1)
    owns = to_chips(given)
    done = [
        sum_of(keep_0[0, 0], got_0[0, 0], *[part[0] for part in parts_0], mirror_0),
        sum_of(keep_1[0, 0], got_1[0], mirror_1, *owns),
    ]
    done = [x.reshape(per_side, per_side, slab_rows, virtuals) for x in done]
    turn = lax.rem(col_index + 1, halves)
    ordered = []
    for half in range(halves):
        value = done[half]
        for other in range(1, halves):
            value = jnp.where(turn == other, done[(half - other) % halves], value)
        ordered.append(value)
    return jnp.where(kept_cells > 0, jnp.concatenate(ordered), 0.0)


def solution(mesh):
    in_specs = (
        P("row", "col", None, None),
        P("row", "col", "vc", None, None),
        P("row", "col"),
        P("row", "col"),
    )
    body = functools.partial(on_device, *(mesh.shape[name] for name in AXES))
    return jax.shard_map(
        body, mesh=mesh, in_specs=in_specs, out_specs=P("row", "col", "vc", None), check_vma=False
    )
```

```python
import functools

import jax
import jax.numpy as jnp
from jax import lax
from jax.experimental import pallas as pl
from jax.experimental.pallas import tpu as pltpu
from jax.sharding import PartitionSpec as P

AXES = ("row", "col", "vc")
CORES = 2
Q_BLOCK = 8
ROWS_LAST = (((1,), (1,)), ((), ()))


def add_blocks(first, last, domain, masked, total, half_a, half_b, rows=None, loaded=None, unroll=False):
    virtuals = domain.shape[1]
    pairs = total.shape[0] // virtuals
    size = half_a.shape[1] // virtuals
    rows = rows or (virtuals,) * (pairs // 2)
    places, end = [], 0
    for pair in range(pairs):
        places.append((pair, end, rows[pair // 2]))
        end += rows[pair // 2]

    def contract(block, half):
        for group, height in enumerate(rows):
            if height == 0:
                continue
            stacked = domain[pl.ds(block * size, size), :height].reshape(size * height, virtuals)
            product = jnp.dot(
                stacked,
                masked[:, 2 * group * virtuals : 2 * (group + 1) * virtuals],
                preferred_element_type=jnp.float32,
            ).astype(jnp.bfloat16)
            for pair, start, _ in places[2 * group : 2 * (group + 1)]:
                lane = (pair - 2 * group) * virtuals
                for q in range(size):
                    half[start : start + height, q * virtuals : (q + 1) * virtuals] = product[
                        q * height : (q + 1) * height, lane : lane + virtuals
                    ]

    def accumulate(block, half):
        slab = domain[pl.ds(block * size, size)]
        beside = jnp.concatenate([slab[q] for q in range(size)], axis=1)
        added = lax.dot_general(
            half[:end], beside, ROWS_LAST, preferred_element_type=jnp.float32
        )
        for pair, start, height in places:
            if height > 0:
                total[pair * virtuals : pair * virtuals + height] += added[start : start + height]

    loaded = loaded or (lambda block: None)
    contract(first, half_a)

    @pl.loop(0, (last - 1 - first) // 2, unroll=unroll)
    def _(i):
        loaded(first + 2 * i + 1)
        loaded(first + 2 * i + 2)
        contract(first + 2 * i + 1, half_b)
        accumulate(first + 2 * i, half_a)
        contract(first + 2 * i + 2, half_a)
        accumulate(first + 2 * i + 1, half_b)

    if (last - 1 - first) % 2:
        loaded(last - 1)
        contract(last - 1, half_b)
        accumulate(last - 2, half_a)
        accumulate(last - 1, half_b)
    else:
        accumulate(last - 1, half_a)


def turn_of(row, col, halves):
    own = jnp.where(lax.div(col, halves) == row, 1, 0)
    return lax.rem(col + own, halves)


def sides_of(pair, pairs):
    bits = (pairs.bit_length() - 1) // 2
    return pair >> bits, pair & ((1 << bits) - 1)


def mirror_place(pair, pairs):
    row, col = sides_of(pair, pairs)
    return (col << ((pairs.bit_length() - 1) // 2)) | row


def split_rows(total, flipped, slabs, outs, order=None):
    virtuals = total.shape[1]
    pairs = total.shape[0] // virtuals
    order = order or range(pairs)
    mirrors = [mirror_place(pair, pairs) for pair in order]
    slab_rows, chips = virtuals // slabs, slabs // CORES
    vc_index = lax.axis_index("vc")
    core, chip = lax.rem(vc_index, CORES), vc_index // CORES
    for pair in range(pairs):
        at = slice(pair * virtuals, (pair + 1) * virtuals)
        flipped[at, :] = total[at, :].T
    for (core_step, chip_step, kind), out in outs.items():
        to_core = core if core_step == 0 else 1 - core
        start = (lax.rem(chip + chip_step, chips) * CORES + to_core) * slab_rows
        for tile, (pair, mirror) in enumerate(zip(order, mirrors)):
            at = pl.ds(pl.multiple_of(tile * virtuals + start, slab_rows), slab_rows)
            if kind == 0:
                out[pair] = total[at, :]
            else:
                out[mirror] = flipped[at, :]


def places_of(core_step, array):
    return {
        (core_step, t, kind): array.at[t, kind] for t in range(array.shape[0]) for kind in range(2)
    }


def first_kernel(
    counts_in, live_in, amps_in, domain_in, keep, give, domain, masked_next,
    counts, live, amps, masked, total, flipped, half_a, half_b, small_sems, domain_sems,
):
    aux, virtuals = domain.shape[:2]
    per_side, row_slots = counts.shape
    pairs = per_side * per_side
    halves = row_slots // per_side
    blocks = aux // Q_BLOCK
    turn = turn_of(lax.axis_index("row"), lax.axis_index("col"), halves)

    def domain_copy(block):
        rows = pl.ds(block * Q_BLOCK, Q_BLOCK)
        return pltpu.make_async_copy(domain_in.at[rows], domain.at[rows], domain_sems.at[block])

    def amps_copy(k):
        rows = pl.ds(lax.rem(turn + k, halves) * per_side, per_side)
        return pltpu.make_async_copy(amps_in.at[rows], amps.at[k], small_sems.at[k])

    def limit(k, pair):
        slot = lax.rem(turn + k, halves) * per_side + pair // per_side
        return jnp.where(live[pair % per_side, slot] > 0, counts[pair % per_side, slot], 0)

    def mask(k, out, limits, order):
        rows = lax.broadcasted_iota(jnp.int32, (virtuals, virtuals), 0)
        cols = lax.broadcasted_iota(jnp.int32, (virtuals, virtuals), 1)
        reach = jnp.maximum(rows, cols)
        for tile, pair in enumerate(order):
            amp = amps[k, *sides_of(pair, pairs)].astype(jnp.float32)
            kept = jnp.where(reach < limits[tile], amp, 0.0)
            out[:, tile * virtuals : (tile + 1) * virtuals] = kept.astype(jnp.bfloat16)

    copies = [
        pltpu.make_async_copy(counts_in, counts, small_sems.at[halves]),
        pltpu.make_async_copy(live_in, live, small_sems.at[halves + 1]),
        *[amps_copy(k) for k in range(halves)],
    ]
    for copy in copies:
        copy.start()
    for block in range(blocks):
        domain_copy(block).start()
    total[...] = jnp.zeros_like(total)
    for copy in copies:
        copy.wait()
    keys = [limit(0, pair) * pairs + pair for pair in range(pairs)]
    for done in range(pairs - 1):
        for i in range(pairs - 1 - done):
            keys[i : i + 2] = jnp.maximum(*keys[i : i + 2]), jnp.minimum(*keys[i : i + 2])
    limits = [key >> (pairs.bit_length() - 1) for key in keys]
    order = [key & (pairs - 1) for key in keys]
    mask(0, masked, limits, order)
    mask(1, masked_next, [limit(1, pair) for pair in range(pairs)], range(pairs))
    domain_copy(0).wait()

    levels = [0, virtuals // 2, 3 * virtuals // 4, virtuals]
    reached = [sum((x > bound).astype(jnp.int32) for bound in levels[:-1]) for x in limits[::2]]
    for high in range(len(levels)):
        for low in range(high + 1):
            @pl.when((reached[0] == high) & (reached[1] == low))
            def _(rows=(levels[high], levels[low])):
                if rows[0] == 0:
                    for block in range(1, blocks):
                        domain_copy(block).wait()
                else:
                    add_blocks(
                        0, blocks, domain, masked, total, half_a, half_b, rows,
                        lambda block: domain_copy(block).wait(),
                    )

    split_rows(
        total, flipped, keep.shape[0] * CORES, {**places_of(0, keep), **places_of(1, give)}, order
    )


def opening_kernel(masked, domain, total, half):
    total[...] = jnp.zeros_like(total)
    add_blocks(0, 1, domain, masked, total, half, half)


def closing_kernel(
    first, masked, total_in, domain, keep, give, give_first, total, flipped, half_a, half_b
):
    chips = keep.shape[0]
    total[...] = total_in[...]
    blocks = domain.shape[0] // Q_BLOCK
    add_blocks(first, blocks, domain, masked, total, half_a, half_b, unroll=True)
    outs = places_of(0, keep)
    for t in range(chips):
        outs[1, t, 0] = give.at[t]
    outs[1, 0, 1] = give.at[chips]
    for t in range(1, chips):
        outs[1, t, 1] = give_first.at[t - 1]
    split_rows(total, flipped, chips * CORES, outs)


def ladder_calls(slabs, counts, live, amps, domain):
    aux, virtuals = domain.shape[:2]
    per_side, row_slots = counts.shape
    pairs = per_side * per_side
    chips = slabs // CORES

    def rows_of(*ahead):
        return jax.ShapeDtypeStruct((*ahead, pairs, virtuals // slabs, virtuals), jnp.float32)

    made = rows_of(chips, 2)
    masked = jax.ShapeDtypeStruct((virtuals, pairs * virtuals), jnp.bfloat16)
    total = jax.ShapeDtypeStruct((pairs * virtuals, virtuals), jnp.float32)

    def half_of(size):
        return jax.ShapeDtypeStruct((pairs * virtuals, size * virtuals), jnp.bfloat16)

    half = half_of(Q_BLOCK)
    vmem = pl.BlockSpec(memory_space=pltpu.VMEM)
    hbm = pl.BlockSpec(memory_space=pltpu.HBM)

    def call(kernel, name, span, in_specs, outs, scratch, more_scratch=()):
        return pl.pallas_call(
            kernel,
            in_specs=in_specs,
            out_specs=[vmem] * len(outs),
            out_shape=outs,
            scratch_shapes=[pltpu.VMEM(x.shape, x.dtype) for x in scratch] + list(more_scratch),
            compiler_params=pltpu.CompilerParams(vmem_limit_bytes=32 * 2**20),
            cost_estimate=pl.CostEstimate(
                flops=4 * pairs * span * Q_BLOCK * virtuals**3,
                bytes_accessed=2 * span * Q_BLOCK * virtuals**2,
                transcendentals=0,
            ),
            name=name,
        )

    def first_half():
        operands = [pltpu.with_memory_space_constraint(x, pltpu.HBM) for x in (counts, live, amps, domain)]

        def kernel(*refs):
            *arrays, counts_here, live_here, small_sems, domain_sems = refs
            first_kernel(*arrays[:8], counts_here, live_here, *arrays[8:], small_sems, domain_sems)

        return call(
            kernel,
            "first_half",
            aux // Q_BLOCK,
            [hbm] * 4,
            [made, made, jax.ShapeDtypeStruct(domain.shape, domain.dtype), masked],
            [
                jax.ShapeDtypeStruct((row_slots // per_side, per_side, *amps.shape[1:]), amps.dtype),
                masked, total, total, half, half,
            ],
            [
                pltpu.SMEM(counts.shape, counts.dtype),
                pltpu.SMEM(live.shape, live.dtype),
                pltpu.SemaphoreType.DMA((row_slots // per_side + 2,)),
                pltpu.SemaphoreType.DMA((aux // Q_BLOCK,)),
            ],
        )(*operands)

    def second_opens(last, masked_1, domain):
        return call(
            opening_kernel, "second_opens", last, [vmem] * 2, [total], [half_of(last * Q_BLOCK)]
        )(masked_1, domain)[0]

    def second_closes(first, masked_1, total_1, domain):
        return call(
            functools.partial(closing_kernel, first),
            "second_closes",
            aux // Q_BLOCK - first,
            [vmem] * 3,
            [made, rows_of(chips + 1), rows_of(chips - 1)],
            [total, total, half, half],
        )(masked_1, total_1, domain)

    return first_half, second_opens, second_closes


def sum_kernel(kind, *refs):
    *parts, out = refs
    out[...] = sum_of(*(part[(0,) * (len(part.shape) - 4) + (kind,)] for part in parts))


def sum_beside(kind, *parts):
    vmem = pl.BlockSpec(memory_space=pltpu.VMEM)
    return pl.pallas_call(
        functools.partial(sum_kernel, kind),
        in_specs=[vmem] * len(parts),
        out_specs=vmem,
        out_shape=jax.ShapeDtypeStruct(parts[0].shape[-3:], jnp.float32),
        compiler_params=pltpu.CompilerParams(vmem_limit_bytes=4 * 2**20),
        cost_estimate=pl.CostEstimate(flops=2**30, bytes_accessed=2**20, transcendentals=0),
        name="sum_beside",
    )(*parts)


def sum_of(*parts):
    return functools.reduce(jnp.add, parts)


def on_device(rows, cols, slabs, amplitudes, factors, pno_counts, pair_live):
    row_slots, per_side = amplitudes.shape[:2]
    halves = row_slots // per_side
    slab_rows, virtuals = amplitudes.shape[2] // slabs, amplitudes.shape[2]
    domain = factors[0, 0]
    row_index, col_index, vc_index = (lax.axis_index(name) for name in AXES)
    reach = jnp.maximum(
        vc_index * slab_rows + lax.broadcasted_iota(jnp.int32, (slab_rows, virtuals), 0),
        lax.broadcasted_iota(jnp.int32, (slab_rows, virtuals), 1),
    )
    limits = jnp.where(pair_live > 0, pno_counts, 0)
    kept_cells = lax.optimization_barrier(
        (reach[None, None] < limits[:, :, None, None]).astype(jnp.float32)
    )

    def send(array, target):
        places = [(r, c, v) for r in range(rows) for c in range(cols) for v in range(slabs)]

        def flat(r, c, v):
            return (r * cols + c) * slabs + v

        return lax.ppermute(array, AXES, [(flat(*place), flat(*target(*place))) for place in places])

    def to_chips(given):
        return [
            send(part, lambda r, c, v, t=t: (r, c, (v + t * CORES) % slabs))
            for t, part in enumerate(given, 1)
        ]

    def mirror_of(k, r, c):
        return c // halves, r * halves + (c + k + (c // halves == r)) % halves

    def to_mirror(k, flipped):
        def target(r, c, v):
            return (r, c, v ^ 1) if mirror_of(k, r, c) == (r, c) else (*mirror_of(k, r, c), v)

        got = send(flipped, target)
        if not any(mirror_of(k, r, c) == (r, c) for r in range(rows) for c in range(cols)):
            return got
        at_row, at_col = mirror_of(k, row_index, col_index)
        return jnp.where((at_row == row_index) & (at_col == col_index), flipped, got)

    tie = lax.optimization_barrier
    opening, chips = 2, slabs // CORES
    assert halves == 2
    first_half, second_opens, second_closes = ladder_calls(slabs, pno_counts.T, pair_live.T, amplitudes, domain)

    def to_core(give):
        return send(give, lambda r, c, v: (r, c, v ^ 1))

    keep_0, give_0, domain, masked_1 = first_half()
    got_0 = to_core(give_0)
    opened = second_opens(opening, masked_1, domain)
    got_0, opened = tie((got_0, opened))
    parts_0 = to_chips([keep_0[t] + got_0[t] for t in range(1, chips)])
    keep_1, give_1, give_first = second_closes(opening, masked_1, opened, domain)
    flipped_0 = sum_beside(1, keep_0, got_0, *parts_0)
    got_first, flipped_0 = tie((to_core(give_first), flipped_0))
    mirror_0 = to_mirror(0, flipped_0)
    given = [keep_1[t, 1] + got_first[t - 1] for t in range(1, chips)]
    flips = to_chips(given)
    got_1 = to_core(tie((give_1, given))[0])
    flipped_1 = sum_of(keep_1[0, 1], got_1[chips], *flips)
    given = [keep_1[t, 0] + got_1[t] for t in range(1, chips)]
    flipped_1, given = tie((flipped_1, given))
    mirror_1 = to_mirror(1, flipped_1)
    owns = to_chips(given)
    done = [
        sum_of(keep_0[0, 0], got_0[0, 0], *[part[0] for part in parts_0], mirror_0),
        sum_of(keep_1[0, 0], got_1[0], *owns, mirror_1),
    ]
    done = [x.reshape(per_side, per_side, slab_rows, virtuals) for x in done]
    turn = turn_of(row_index, col_index, halves)
    ordered = []
    for half in range(halves):
        value = done[half]
        for other in range(1, halves):
            value = jnp.where(turn == other, done[(half - other) % halves], value)
        ordered.append(value)
    return jnp.where(kept_cells > 0, jnp.concatenate(ordered), 0.0)


def solution(mesh):
    in_specs = (
        P("row", "col", None, None),
        P("row", "col", "vc", None, None),
        P("row", "col"),
        P("row", "col"),
    )
    body = functools.partial(on_device, *(mesh.shape[name] for name in AXES))
    return jax.shard_map(
        body, mesh=mesh, in_specs=in_specs, out_specs=P("row", "col", "vc", None), check_vma=False
    )
```

```python
import functools

import jax
import jax.numpy as jnp
from jax import lax
from jax.experimental import pallas as pl
from jax.experimental.pallas import tpu as pltpu
from jax.sharding import PartitionSpec as P

AXES = ("row", "col", "vc")
CORES = 2
Q_BLOCK = 8
ROWS_LAST = (((1,), (1,)), ((), ()))


def add_blocks(first, last, domain, masked, total, half_a, half_b, rows=None, loaded=None, unroll=False):
    virtuals = domain.shape[1]
    pairs = total.shape[0] // virtuals
    size = half_a.shape[1] // virtuals
    rows = rows or (virtuals,) * (pairs // 2)
    places, end = [], 0
    for pair in range(pairs):
        places.append((pair, end, rows[pair // 2]))
        end += rows[pair // 2]

    def contract(block, half):
        for group, height in enumerate(rows):
            if height == 0:
                continue
            stacked = domain[pl.ds(block * size, size), :height].reshape(size * height, virtuals)
            product = jnp.dot(
                stacked,
                masked[:, 2 * group * virtuals : 2 * (group + 1) * virtuals],
                preferred_element_type=jnp.float32,
            ).astype(jnp.bfloat16)
            for pair, start, _ in places[2 * group : 2 * (group + 1)]:
                lane = (pair - 2 * group) * virtuals
                for q in range(size):
                    half[start : start + height, q * virtuals : (q + 1) * virtuals] = product[
                        q * height : (q + 1) * height, lane : lane + virtuals
                    ]

    def accumulate(block, half):
        slab = domain[pl.ds(block * size, size)]
        beside = jnp.concatenate([slab[q] for q in range(size)], axis=1)
        added = lax.dot_general(
            half[:end], beside, ROWS_LAST, preferred_element_type=jnp.float32
        )
        for pair, start, height in places:
            if height > 0:
                total[pair * virtuals : pair * virtuals + height] += added[start : start + height]

    loaded = loaded or (lambda block: None)
    contract(first, half_a)

    @pl.loop(0, (last - 1 - first) // 2, unroll=unroll)
    def _(i):
        loaded(first + 2 * i + 1)
        loaded(first + 2 * i + 2)
        contract(first + 2 * i + 1, half_b)
        accumulate(first + 2 * i, half_a)
        contract(first + 2 * i + 2, half_a)
        accumulate(first + 2 * i + 1, half_b)

    if (last - 1 - first) % 2:
        loaded(last - 1)
        contract(last - 1, half_b)
        accumulate(last - 2, half_a)
        accumulate(last - 1, half_b)
    else:
        accumulate(last - 1, half_a)


def turn_of(row, col, halves):
    own = jnp.where(lax.div(col, halves) == row, 1, 0)
    return lax.rem(col + own, halves)


def sides_of(pair, pairs):
    bits = (pairs.bit_length() - 1) // 2
    return pair >> bits, pair & ((1 << bits) - 1)


def mirror_place(pair, pairs):
    row, col = sides_of(pair, pairs)
    return (col << ((pairs.bit_length() - 1) // 2)) | row


def split_rows(total, flipped, slabs, outs, order=None):
    virtuals = total.shape[1]
    pairs = total.shape[0] // virtuals
    order = order or range(pairs)
    mirrors = [mirror_place(pair, pairs) for pair in order]
    slab_rows, chips = virtuals // slabs, slabs // CORES
    vc_index = lax.axis_index("vc")
    core, chip = lax.rem(vc_index, CORES), vc_index // CORES
    for pair in range(pairs):
        at = slice(pair * virtuals, (pair + 1) * virtuals)
        flipped[at, :] = total[at, :].T
    for (core_step, chip_step, kind), out in outs.items():
        to_core = core if core_step == 0 else 1 - core
        start = (lax.rem(chip + chip_step, chips) * CORES + to_core) * slab_rows
        for tile, (pair, mirror) in enumerate(zip(order, mirrors)):
            at = pl.ds(pl.multiple_of(tile * virtuals + start, slab_rows), slab_rows)
            if kind == 0:
                out[pair] = total[at, :]
            else:
                out[mirror] = flipped[at, :]


def places_of(core_step, array):
    return {
        (core_step, t, kind): array.at[t, kind] for t in range(array.shape[0]) for kind in range(2)
    }


def first_kernel(
    counts_in, live_in, amps_in, domain_in, keep, give, domain, masked_next,
    counts, live, amps, masked, total, flipped, half_a, half_b, small_sems, domain_sems,
):
    aux, virtuals = domain.shape[:2]
    per_side, row_slots = counts.shape
    pairs = per_side * per_side
    halves = row_slots // per_side
    blocks = aux // Q_BLOCK
    turn = turn_of(lax.axis_index("row"), lax.axis_index("col"), halves)

    def domain_copy(block):
        rows = pl.ds(block * Q_BLOCK, Q_BLOCK)
        return pltpu.make_async_copy(domain_in.at[rows], domain.at[rows], domain_sems.at[block])

    def amps_copy(k):
        rows = pl.ds(lax.rem(turn + k, halves) * per_side, per_side)
        return pltpu.make_async_copy(amps_in.at[rows], amps.at[k], small_sems.at[k])

    def limit(k, pair):
        slot = lax.rem(turn + k, halves) * per_side + pair // per_side
        return jnp.where(live[pair % per_side, slot] > 0, counts[pair % per_side, slot], 0)

    def mask(k, out, limits, order):
        rows = lax.broadcasted_iota(jnp.int32, (virtuals, virtuals), 0)
        cols = lax.broadcasted_iota(jnp.int32, (virtuals, virtuals), 1)
        reach = jnp.maximum(rows, cols)
        for tile, pair in enumerate(order):
            amp = amps[k, *sides_of(pair, pairs)].astype(jnp.float32)
            kept = jnp.where(reach < limits[tile], amp, 0.0)
            out[:, tile * virtuals : (tile + 1) * virtuals] = kept.astype(jnp.bfloat16)

    copies = [
        pltpu.make_async_copy(counts_in, counts, small_sems.at[halves]),
        pltpu.make_async_copy(live_in, live, small_sems.at[halves + 1]),
        *[amps_copy(k) for k in range(halves)],
    ]
    for copy in copies:
        copy.start()
    for block in range(blocks):
        domain_copy(block).start()
    total[...] = jnp.zeros_like(total)
    for copy in copies:
        copy.wait()
    keys = [limit(0, pair) * pairs + pair for pair in range(pairs)]
    for done in range(pairs - 1):
        for i in range(pairs - 1 - done):
            keys[i : i + 2] = jnp.maximum(*keys[i : i + 2]), jnp.minimum(*keys[i : i + 2])
    limits = [key >> (pairs.bit_length() - 1) for key in keys]
    order = [key & (pairs - 1) for key in keys]
    mask(0, masked, limits, order)
    mask(1, masked_next, [limit(1, pair) for pair in range(pairs)], range(pairs))
    domain_copy(0).wait()

    levels = [0, virtuals // 2, 3 * virtuals // 4, virtuals]
    reached = [sum((x > bound).astype(jnp.int32) for bound in levels[:-1]) for x in limits[::2]]
    for high in range(len(levels)):
        for low in range(high + 1):
            @pl.when((reached[0] == high) & (reached[1] == low))
            def _(rows=(levels[high], levels[low])):
                if rows[0] == 0:
                    for block in range(1, blocks):
                        domain_copy(block).wait()
                else:
                    add_blocks(
                        0, blocks, domain, masked, total, half_a, half_b, rows,
                        lambda block: domain_copy(block).wait(),
                    )

    split_rows(
        total, flipped, keep.shape[0] * CORES, {**places_of(0, keep), **places_of(1, give)}, order
    )


def opening_kernel(masked, domain, total, half):
    total[...] = jnp.zeros_like(total)
    add_blocks(0, 1, domain, masked, total, half, half)


def closing_kernel(
    first, masked, total_in, domain, keep, give, give_first, total, flipped, half_a, half_b
):
    chips = keep.shape[0]
    total[...] = total_in[...]
    blocks = domain.shape[0] // Q_BLOCK
    add_blocks(first, blocks, domain, masked, total, half_a, half_b, unroll=True)
    outs = places_of(0, keep)
    for t in range(chips):
        outs[1, t, 0] = give.at[t]
    outs[1, 0, 1] = give.at[chips]
    for t in range(1, chips):
        outs[1, t, 1] = give_first.at[t - 1]
    split_rows(total, flipped, chips * CORES, outs)


def ladder_calls(slabs, counts, live, amps, domain):
    aux, virtuals = domain.shape[:2]
    per_side, row_slots = counts.shape
    pairs = per_side * per_side
    chips = slabs // CORES

    def rows_of(*ahead):
        return jax.ShapeDtypeStruct((*ahead, pairs, virtuals // slabs, virtuals), jnp.float32)

    made = rows_of(chips, 2)
    masked = jax.ShapeDtypeStruct((virtuals, pairs * virtuals), jnp.bfloat16)
    total = jax.ShapeDtypeStruct((pairs * virtuals, virtuals), jnp.float32)

    def half_of(size):
        return jax.ShapeDtypeStruct((pairs * virtuals, size * virtuals), jnp.bfloat16)

    half = half_of(Q_BLOCK)
    vmem = pl.BlockSpec(memory_space=pltpu.VMEM)
    hbm = pl.BlockSpec(memory_space=pltpu.HBM)

    def call(kernel, name, span, in_specs, outs, scratch, more_scratch=()):
        return pl.pallas_call(
            kernel,
            in_specs=in_specs,
            out_specs=[vmem] * len(outs),
            out_shape=outs,
            scratch_shapes=[pltpu.VMEM(x.shape, x.dtype) for x in scratch] + list(more_scratch),
            compiler_params=pltpu.CompilerParams(vmem_limit_bytes=32 * 2**20),
            cost_estimate=pl.CostEstimate(
                flops=4 * pairs * span * Q_BLOCK * virtuals**3,
                bytes_accessed=2 * span * Q_BLOCK * virtuals**2,
                transcendentals=0,
            ),
            name=name,
        )

    def first_half():
        operands = [pltpu.with_memory_space_constraint(x, pltpu.HBM) for x in (counts, live, amps, domain)]

        def kernel(*refs):
            *arrays, counts_here, live_here, small_sems, domain_sems = refs
            first_kernel(*arrays[:8], counts_here, live_here, *arrays[8:], small_sems, domain_sems)

        return call(
            kernel,
            "first_half",
            aux // Q_BLOCK,
            [hbm] * 4,
            [made, made, jax.ShapeDtypeStruct(domain.shape, domain.dtype), masked],
            [
                jax.ShapeDtypeStruct((row_slots // per_side, per_side, *amps.shape[1:]), amps.dtype),
                masked, total, total, half, half,
            ],
            [
                pltpu.SMEM(counts.shape, counts.dtype),
                pltpu.SMEM(live.shape, live.dtype),
                pltpu.SemaphoreType.DMA((row_slots // per_side + 2,)),
                pltpu.SemaphoreType.DMA((aux // Q_BLOCK,)),
            ],
        )(*operands)

    def second_opens(last, masked_1, domain):
        return call(
            opening_kernel, "second_opens", last, [vmem] * 2, [total], [half_of(last * Q_BLOCK)]
        )(masked_1, domain)[0]

    def second_closes(first, masked_1, total_1, domain):
        return call(
            functools.partial(closing_kernel, first),
            "second_closes",
            aux // Q_BLOCK - first,
            [vmem] * 3,
            [made, rows_of(chips + 1), rows_of(chips - 1)],
            [total, total, half, half],
        )(masked_1, total_1, domain)

    return first_half, second_opens, second_closes


def sum_kernel(kind, *refs):
    *parts, out = refs
    out[...] = sum_of(*(part[(0,) * (len(part.shape) - 4) + (kind,)] for part in parts))


def sum_beside(kind, *parts):
    vmem = pl.BlockSpec(memory_space=pltpu.VMEM)
    return pl.pallas_call(
        functools.partial(sum_kernel, kind),
        in_specs=[vmem] * len(parts),
        out_specs=vmem,
        out_shape=jax.ShapeDtypeStruct(parts[0].shape[-3:], jnp.float32),
        compiler_params=pltpu.CompilerParams(vmem_limit_bytes=4 * 2**20),
        cost_estimate=pl.CostEstimate(flops=2**30, bytes_accessed=2**20, transcendentals=0),
        name="sum_beside",
    )(*parts)


def sum_of(*parts):
    return functools.reduce(jnp.add, parts)


def on_device(rows, cols, slabs, amplitudes, factors, pno_counts, pair_live):
    row_slots, per_side = amplitudes.shape[:2]
    halves = row_slots // per_side
    slab_rows, virtuals = amplitudes.shape[2] // slabs, amplitudes.shape[2]
    domain = factors[0, 0]
    row_index, col_index, vc_index = (lax.axis_index(name) for name in AXES)
    reach = jnp.maximum(
        vc_index * slab_rows + lax.broadcasted_iota(jnp.int32, (slab_rows, virtuals), 0),
        lax.broadcasted_iota(jnp.int32, (slab_rows, virtuals), 1),
    )
    limits = jnp.where(pair_live > 0, pno_counts, 0)
    kept_cells = lax.optimization_barrier(
        (reach[None, None] < limits[:, :, None, None]).astype(jnp.float32)
    )

    def send(array, target):
        places = [(r, c, v) for r in range(rows) for c in range(cols) for v in range(slabs)]

        def flat(r, c, v):
            return (r * cols + c) * slabs + v

        return lax.ppermute(array, AXES, [(flat(*place), flat(*target(*place))) for place in places])

    def to_chips(given):
        return [
            send(part, lambda r, c, v, t=t: (r, c, (v + t * CORES) % slabs))
            for t, part in enumerate(given, 1)
        ]

    def mirror_of(k, r, c):
        return c // halves, r * halves + (c + k + (c // halves == r)) % halves

    def to_mirror(k, flipped):
        def target(r, c, v):
            return (r, c, v ^ 1) if mirror_of(k, r, c) == (r, c) else (*mirror_of(k, r, c), v)

        got = send(flipped, target)
        if not any(mirror_of(k, r, c) == (r, c) for r in range(rows) for c in range(cols)):
            return got
        at_row, at_col = mirror_of(k, row_index, col_index)
        return jnp.where((at_row == row_index) & (at_col == col_index), flipped, got)

    tie = lax.optimization_barrier
    opening, chips = 2, slabs // CORES
    assert halves == 2
    first_half, second_opens, second_closes = ladder_calls(slabs, pno_counts.T, pair_live.T, amplitudes, domain)

    def to_core(give):
        return send(give, lambda r, c, v: (r, c, v ^ 1))

    keep_0, give_0, domain, masked_1 = first_half()
    got_0 = to_core(give_0)
    opened = second_opens(opening, masked_1, domain)
    got_0, opened = tie((got_0, opened))
    parts_0 = to_chips([keep_0[t] + got_0[t] for t in range(1, chips)])
    keep_1, give_1, give_first = second_closes(opening, masked_1, opened, domain)
    flipped_0 = sum_beside(1, keep_0, got_0, *parts_0)
    got_first, flipped_0 = tie((to_core(give_first), flipped_0))
    mirror_0 = to_mirror(0, flipped_0)
    given = [keep_1[t, 1] + got_first[t - 1] for t in range(1, chips)]
    flips = to_chips(given)
    got_1 = to_core(tie((give_1, given))[0])
    given = [keep_1[t, 0] + got_1[t] for t in range(1, chips)]
    held = sum_beside(0, tie((keep_1[0, 1] + got_1[chips], given))[0][None])
    flipped_1 = sum_of(held, *flips)
    mirror_1 = to_mirror(1, flipped_1)
    owns = to_chips(given)
    done = [
        sum_of(keep_0[0, 0], got_0[0, 0], *[part[0] for part in parts_0], mirror_0),
        sum_of(keep_1[0, 0], got_1[0], mirror_1, *owns),
    ]
    done = [x.reshape(per_side, per_side, slab_rows, virtuals) for x in done]
    turn = turn_of(row_index, col_index, halves)
    ordered = []
    for half in range(halves):
        value = done[half]
        for other in range(1, halves):
            value = jnp.where(turn == other, done[(half - other) % halves], value)
        ordered.append(value)
    return jnp.where(kept_cells > 0, jnp.concatenate(ordered), 0.0)


def solution(mesh):
    in_specs = (
        P("row", "col", None, None),
        P("row", "col", "vc", None, None),
        P("row", "col"),
        P("row", "col"),
    )
    body = functools.partial(on_device, *(mesh.shape[name] for name in AXES))
    return jax.shard_map(
        body, mesh=mesh, in_specs=in_specs, out_specs=P("row", "col", "vc", None), check_vma=False
    )
```

```python
import functools

import jax
import jax.numpy as jnp
from jax import lax
from jax.experimental import pallas as pl
from jax.experimental.pallas import tpu as pltpu
from jax.sharding import PartitionSpec as P

AXES = ("row", "col", "vc")
CORES = 2
Q_BLOCK = 8
ROWS_LAST = (((1,), (1,)), ((), ()))


def add_blocks(first, last, domain, masked, total, half_a, half_b, rows=None, loaded=None, unroll=False):
    virtuals = domain.shape[1]
    pairs = total.shape[0] // virtuals
    size = half_a.shape[1] // virtuals
    rows = rows or (virtuals,) * (pairs // 2)
    places, end = [], 0
    for pair in range(pairs):
        places.append((pair, end, rows[pair // 2]))
        end += rows[pair // 2]

    def contract(block, half):
        for group, height in enumerate(rows):
            if height == 0:
                continue
            stacked = domain[pl.ds(block * size, size), :height].reshape(size * height, virtuals)
            product = jnp.dot(
                stacked,
                masked[:, 2 * group * virtuals : 2 * (group + 1) * virtuals],
                preferred_element_type=jnp.float32,
            ).astype(jnp.bfloat16)
            for pair, start, _ in places[2 * group : 2 * (group + 1)]:
                lane = (pair - 2 * group) * virtuals
                for q in range(size):
                    half[start : start + height, q * virtuals : (q + 1) * virtuals] = product[
                        q * height : (q + 1) * height, lane : lane + virtuals
                    ]

    def accumulate(block, half):
        slab = domain[pl.ds(block * size, size)]
        beside = jnp.concatenate([slab[q] for q in range(size)], axis=1)
        added = lax.dot_general(
            half[:end], beside, ROWS_LAST, preferred_element_type=jnp.float32
        )
        for pair, start, height in places:
            if height > 0:
                total[pair * virtuals : pair * virtuals + height] += added[start : start + height]

    loaded = loaded or (lambda block: None)
    contract(first, half_a)

    @pl.loop(0, (last - 1 - first) // 2, unroll=unroll)
    def _(i):
        loaded(first + 2 * i + 1)
        loaded(first + 2 * i + 2)
        contract(first + 2 * i + 1, half_b)
        accumulate(first + 2 * i, half_a)
        contract(first + 2 * i + 2, half_a)
        accumulate(first + 2 * i + 1, half_b)

    if (last - 1 - first) % 2:
        loaded(last - 1)
        contract(last - 1, half_b)
        accumulate(last - 2, half_a)
        accumulate(last - 1, half_b)
    else:
        accumulate(last - 1, half_a)


def turn_of(row, col, halves):
    own = jnp.where(lax.div(col, halves) == row, 1, 0)
    return lax.rem(col + own, halves)


def sides_of(pair, pairs):
    bits = (pairs.bit_length() - 1) // 2
    return pair >> bits, pair & ((1 << bits) - 1)


def mirror_place(pair, pairs):
    row, col = sides_of(pair, pairs)
    return (col << ((pairs.bit_length() - 1) // 2)) | row


def split_rows(total, flipped, slabs, outs, order=None):
    virtuals = total.shape[1]
    pairs = total.shape[0] // virtuals
    order = order or range(pairs)
    mirrors = [mirror_place(pair, pairs) for pair in order]
    slab_rows, chips = virtuals // slabs, slabs // CORES
    vc_index = lax.axis_index("vc")
    core, chip = lax.rem(vc_index, CORES), vc_index // CORES
    for pair in range(pairs):
        at = slice(pair * virtuals, (pair + 1) * virtuals)
        flipped[at, :] = total[at, :].T
    for (core_step, chip_step, kind), out in outs.items():
        to_core = core if core_step == 0 else 1 - core
        start = (lax.rem(chip + chip_step, chips) * CORES + to_core) * slab_rows
        for tile, (pair, mirror) in enumerate(zip(order, mirrors)):
            at = pl.ds(pl.multiple_of(tile * virtuals + start, slab_rows), slab_rows)
            if kind == 0:
                out[pair] = total[at, :]
            else:
                out[mirror] = flipped[at, :]


def places_of(core_step, array):
    return {
        (core_step, t, kind): array.at[t, kind] for t in range(array.shape[0]) for kind in range(2)
    }


def row_levels(virtuals, k):
    return [0, virtuals // 2, 3 * virtuals // 4, virtuals] if k == 0 else [0, virtuals // 2, virtuals]


def by_rows(reached, levels, run):
    for high in range(len(levels)):
        for low in range(high + 1):
            @pl.when((reached[0] == high) & (reached[1] == low))
            def _(rows=(levels[high], levels[low])):
                run(rows)


def first_kernel(
    counts_in, live_in, amps_in, domain_in, keep, give, domain, masked_next, code,
    counts, live, amps, masked, total, flipped, half_a, half_b, small_sems, domain_sems,
):
    aux, virtuals = domain.shape[:2]
    per_side, row_slots = counts.shape
    pairs = per_side * per_side
    halves = row_slots // per_side
    blocks = aux // Q_BLOCK
    turn = turn_of(lax.axis_index("row"), lax.axis_index("col"), halves)

    def domain_copy(block):
        rows = pl.ds(block * Q_BLOCK, Q_BLOCK)
        return pltpu.make_async_copy(domain_in.at[rows], domain.at[rows], domain_sems.at[block])

    def amps_copy(k):
        rows = pl.ds(lax.rem(turn + k, halves) * per_side, per_side)
        return pltpu.make_async_copy(amps_in.at[rows], amps.at[k], small_sems.at[k])

    def limit(k, pair):
        slot = lax.rem(turn + k, halves) * per_side + pair // per_side
        return jnp.where(live[pair % per_side, slot] > 0, counts[pair % per_side, slot], 0)

    def mask(k, out, limits, order):
        rows = lax.broadcasted_iota(jnp.int32, (virtuals, virtuals), 0)
        cols = lax.broadcasted_iota(jnp.int32, (virtuals, virtuals), 1)
        reach = jnp.maximum(rows, cols)
        for tile, pair in enumerate(order):
            amp = amps[k, *sides_of(pair, pairs)].astype(jnp.float32)
            kept = jnp.where(reach < limits[tile], amp, 0.0)
            out[:, tile * virtuals : (tile + 1) * virtuals] = kept.astype(jnp.bfloat16)

    copies = [
        pltpu.make_async_copy(counts_in, counts, small_sems.at[halves]),
        pltpu.make_async_copy(live_in, live, small_sems.at[halves + 1]),
        *[amps_copy(k) for k in range(halves)],
    ]
    for copy in copies:
        copy.start()
    for block in range(blocks):
        domain_copy(block).start()
    total[...] = jnp.zeros_like(total)
    for copy in copies:
        copy.wait()
    bits = pairs.bit_length() - 1

    def by_count(k):
        keys = [limit(k, pair) * pairs + pair for pair in range(pairs)]
        for done in range(pairs - 1):
            for i in range(pairs - 1 - done):
                keys[i : i + 2] = jnp.maximum(*keys[i : i + 2]), jnp.minimum(*keys[i : i + 2])
        limits = [key >> bits for key in keys]
        bounds = row_levels(virtuals, k)[:-1]
        reached = [sum((x > bound).astype(jnp.int32) for bound in bounds) for x in limits[::2]]
        return limits, [key & (pairs - 1) for key in keys], reached

    limits, order, reached = by_count(0)
    mask(0, masked, limits, order)
    limits_next, order_next, reached_next = by_count(1)
    mask(1, masked_next, limits_next, order_next)
    number = sum(x << (bits * i) for i, x in enumerate([*reached_next, *order_next]))
    code[...] = jnp.full(code.shape, number.astype(jnp.float32))
    domain_copy(0).wait()

    def run(rows):
        if rows[0] == 0:
            for block in range(1, blocks):
                domain_copy(block).wait()
        else:
            add_blocks(
                0, blocks, domain, masked, total, half_a, half_b, rows,
                lambda block: domain_copy(block).wait(),
            )

    by_rows(reached, row_levels(virtuals, 0), run)
    split_rows(
        total, flipped, keep.shape[0] * CORES, {**places_of(0, keep), **places_of(1, give)}, order
    )


def read_code(code, pairs):
    bits = pairs.bit_length() - 1
    number = jnp.max(code[...]).astype(jnp.int32)
    fields = [(number >> (bits * i)) & (pairs - 1) for i in range(2 + pairs)]
    return fields[:2], fields[2:]


def opening_kernel(code, masked, domain, total, half):
    virtuals = domain.shape[1]
    reached, _ = read_code(code, total.shape[0] // virtuals)
    total[...] = jnp.zeros_like(total)

    def run(rows):
        if rows[0] > 0:
            add_blocks(0, 1, domain, masked, total, half, half, rows)

    by_rows(reached, row_levels(virtuals, 1), run)


def closing_kernel(
    first, code, masked, total_in, domain, keep, give, give_first, total, flipped, half_a, half_b
):
    chips = keep.shape[0]
    virtuals = domain.shape[1]
    reached, order = read_code(code, total.shape[0] // virtuals)
    total[...] = total_in[...]

    def run(rows):
        if rows[0] > 0:
            blocks = domain.shape[0] // Q_BLOCK
            add_blocks(first, blocks, domain, masked, total, half_a, half_b, rows, unroll=True)

    by_rows(reached, row_levels(virtuals, 1), run)
    outs = places_of(0, keep)
    for t in range(chips):
        outs[1, t, 0] = give.at[t]
    outs[1, 0, 1] = give.at[chips]
    for t in range(1, chips):
        outs[1, t, 1] = give_first.at[t - 1]
    split_rows(total, flipped, chips * CORES, outs, order)


def ladder_calls(slabs, counts, live, amps, domain):
    aux, virtuals = domain.shape[:2]
    per_side, row_slots = counts.shape
    pairs = per_side * per_side
    chips = slabs // CORES

    def rows_of(*ahead):
        return jax.ShapeDtypeStruct((*ahead, pairs, virtuals // slabs, virtuals), jnp.float32)

    made = rows_of(chips, 2)
    masked = jax.ShapeDtypeStruct((virtuals, pairs * virtuals), jnp.bfloat16)
    total = jax.ShapeDtypeStruct((pairs * virtuals, virtuals), jnp.float32)
    code = jax.ShapeDtypeStruct((8, 128), jnp.float32)

    def half_of(size):
        return jax.ShapeDtypeStruct((pairs * virtuals, size * virtuals), jnp.bfloat16)

    half = half_of(Q_BLOCK)
    vmem = pl.BlockSpec(memory_space=pltpu.VMEM)
    hbm = pl.BlockSpec(memory_space=pltpu.HBM)

    def call(kernel, name, span, in_specs, outs, scratch, more_scratch=()):
        return pl.pallas_call(
            kernel,
            in_specs=in_specs,
            out_specs=[vmem] * len(outs),
            out_shape=outs,
            scratch_shapes=[pltpu.VMEM(x.shape, x.dtype) for x in scratch] + list(more_scratch),
            compiler_params=pltpu.CompilerParams(vmem_limit_bytes=32 * 2**20),
            cost_estimate=pl.CostEstimate(
                flops=4 * pairs * span * Q_BLOCK * virtuals**3,
                bytes_accessed=2 * span * Q_BLOCK * virtuals**2,
                transcendentals=0,
            ),
            name=name,
        )

    def first_half():
        operands = [pltpu.with_memory_space_constraint(x, pltpu.HBM) for x in (counts, live, amps, domain)]

        def kernel(*refs):
            *arrays, counts_here, live_here, small_sems, domain_sems = refs
            first_kernel(*arrays[:9], counts_here, live_here, *arrays[9:], small_sems, domain_sems)

        return call(
            kernel,
            "first_half",
            aux // Q_BLOCK,
            [hbm] * 4,
            [made, made, jax.ShapeDtypeStruct(domain.shape, domain.dtype), masked, code],
            [
                jax.ShapeDtypeStruct((row_slots // per_side, per_side, *amps.shape[1:]), amps.dtype),
                masked, total, total, half, half,
            ],
            [
                pltpu.SMEM(counts.shape, counts.dtype),
                pltpu.SMEM(live.shape, live.dtype),
                pltpu.SemaphoreType.DMA((row_slots // per_side + 2,)),
                pltpu.SemaphoreType.DMA((aux // Q_BLOCK,)),
            ],
        )(*operands)

    def second_opens(last, code_1, masked_1, domain):
        return call(
            opening_kernel, "second_opens", last, [vmem] * 3, [total], [half_of(last * Q_BLOCK)]
        )(code_1, masked_1, domain)[0]

    def second_closes(first, code_1, masked_1, total_1, domain):
        return call(
            functools.partial(closing_kernel, first),
            "second_closes",
            aux // Q_BLOCK - first,
            [vmem] * 4,
            [made, rows_of(chips + 1), rows_of(chips - 1)],
            [total, total, half, half],
        )(code_1, masked_1, total_1, domain)

    return first_half, second_opens, second_closes


def sum_kernel(kind, *refs):
    *parts, out = refs
    out[...] = sum_of(*(part[(0,) * (len(part.shape) - 4) + (kind,)] for part in parts))


def sum_beside(kind, *parts):
    vmem = pl.BlockSpec(memory_space=pltpu.VMEM)
    return pl.pallas_call(
        functools.partial(sum_kernel, kind),
        in_specs=[vmem] * len(parts),
        out_specs=vmem,
        out_shape=jax.ShapeDtypeStruct(parts[0].shape[-3:], jnp.float32),
        compiler_params=pltpu.CompilerParams(vmem_limit_bytes=4 * 2**20),
        cost_estimate=pl.CostEstimate(flops=2**30, bytes_accessed=2**20, transcendentals=0),
        name="sum_beside",
    )(*parts)


def sum_of(*parts):
    return functools.reduce(jnp.add, parts)


def on_device(rows, cols, slabs, amplitudes, factors, pno_counts, pair_live):
    row_slots, per_side = amplitudes.shape[:2]
    halves = row_slots // per_side
    slab_rows, virtuals = amplitudes.shape[2] // slabs, amplitudes.shape[2]
    domain = factors[0, 0]
    row_index, col_index, vc_index = (lax.axis_index(name) for name in AXES)
    reach = jnp.maximum(
        vc_index * slab_rows + lax.broadcasted_iota(jnp.int32, (slab_rows, virtuals), 0),
        lax.broadcasted_iota(jnp.int32, (slab_rows, virtuals), 1),
    )
    limits = jnp.where(pair_live > 0, pno_counts, 0)
    kept_cells = lax.optimization_barrier(
        (reach[None, None] < limits[:, :, None, None]).astype(jnp.float32)
    )

    def send(array, target):
        places = [(r, c, v) for r in range(rows) for c in range(cols) for v in range(slabs)]

        def flat(r, c, v):
            return (r * cols + c) * slabs + v

        return lax.ppermute(array, AXES, [(flat(*place), flat(*target(*place))) for place in places])

    def to_chips(given):
        return [
            send(part, lambda r, c, v, t=t: (r, c, (v + t * CORES) % slabs))
            for t, part in enumerate(given, 1)
        ]

    def mirror_of(k, r, c):
        return c // halves, r * halves + (c + k + (c // halves == r)) % halves

    def to_mirror(k, flipped):
        def target(r, c, v):
            return (r, c, v ^ 1) if mirror_of(k, r, c) == (r, c) else (*mirror_of(k, r, c), v)

        got = send(flipped, target)
        if not any(mirror_of(k, r, c) == (r, c) for r in range(rows) for c in range(cols)):
            return got
        at_row, at_col = mirror_of(k, row_index, col_index)
        return jnp.where((at_row == row_index) & (at_col == col_index), flipped, got)

    tie = lax.optimization_barrier
    opening, chips = 2, slabs // CORES
    assert halves == 2
    first_half, second_opens, second_closes = ladder_calls(slabs, pno_counts.T, pair_live.T, amplitudes, domain)

    def to_core(give):
        return send(give, lambda r, c, v: (r, c, v ^ 1))

    keep_0, give_0, domain, masked_1, code_1 = first_half()
    got_0 = to_core(give_0)
    opened = second_opens(opening, code_1, masked_1, domain)
    got_0, opened = tie((got_0, opened))
    parts_0 = to_chips([keep_0[t] + got_0[t] for t in range(1, chips)])
    keep_1, give_1, give_first = second_closes(opening, code_1, masked_1, opened, domain)
    flipped_0 = sum_beside(1, keep_0, got_0, *parts_0)
    got_first, flipped_0 = tie((to_core(give_first), flipped_0))
    mirror_0 = to_mirror(0, flipped_0)
    given = [keep_1[t, 1] + got_first[t - 1] for t in range(1, chips)]
    flips = to_chips(given)
    got_1 = to_core(tie((give_1, given))[0])
    given = [keep_1[t, 0] + got_1[t] for t in range(1, chips)]
    held = sum_beside(0, tie((keep_1[0, 1] + got_1[chips], given))[0][None])
    flipped_1 = sum_of(held, *flips)
    mirror_1 = to_mirror(1, flipped_1)
    owns = to_chips(given)
    done = [
        sum_of(keep_0[0, 0], got_0[0, 0], *[part[0] for part in parts_0], mirror_0),
        sum_of(keep_1[0, 0], got_1[0], mirror_1, *owns),
    ]
    done = [x.reshape(per_side, per_side, slab_rows, virtuals) for x in done]
    turn = turn_of(row_index, col_index, halves)
    ordered = []
    for half in range(halves):
        value = done[half]
        for other in range(1, halves):
            value = jnp.where(turn == other, done[(half - other) % halves], value)
        ordered.append(value)
    return jnp.where(kept_cells > 0, jnp.concatenate(ordered), 0.0)


def solution(mesh):
    in_specs = (
        P("row", "col", None, None),
        P("row", "col", "vc", None, None),
        P("row", "col"),
        P("row", "col"),
    )
    body = functools.partial(on_device, *(mesh.shape[name] for name in AXES))
    return jax.shard_map(
        body, mesh=mesh, in_specs=in_specs, out_specs=P("row", "col", "vc", None), check_vma=False
    )
```
